32 devices in a mesh: gx: 8 (over z, y), gy: 4 (over x, core).
Axes of the slice: x: 2, y: 2, z: 4, core: 2. Of those that a mesh axis runs over, the one named last changes fastest.
Arguments:
- stream: bfloat16 [64, 18432], P(('gx', 'gy')), may hold values from -6 to 6
- norm_gain: float32 [18432], replicated, may hold values from 0.1 to 1.9
- w_gate: bfloat16 [18432, 36864], P('gx', 'gy'), may hold values from -0.046875 to 0.046875
- w_up: bfloat16 [18432, 36864], P('gx', 'gy'), may hold values from -0.046875 to 0.046875
- w_query: bfloat16 [18432, 6144], P('gx', 'gy'), may hold values from -0.046875 to 0.046875
- w_keyval: bfloat16 [18432, 512], P('gx', 'gy'), may hold values from -0.046875 to 0.046875
- k_cache: bfloat16 [64, 512, 256], P(('gx', 'gy')), may hold values from -200 to 200
- v_cache: bfloat16 [64, 512, 256], P(('gx', 'gy')), may hold values from -6 to 6
- lengths: int32 [64], P(('gx', 'gy')), may hold values from 1 to 512, 16384 in all
Outputs:
- hidden: bfloat16 [64, 36864], P('gx', 'gy')
- context: bfloat16 [64, 6144], P(('gx', 'gy'))
The draws below stay inside these ranges and needn't reach their ends.
Inputs may be any that keep to these rules, and one draw needn't show every extreme that they name: `lengths`: some row has 512 filled slots.
All inputs are finite; a program needn't handle non-finite values. No bound on the sum of `lengths` on one device may be relied on, other than what follows from the above.
Results may differ from the reference program's by a relative error of at most 0.017.
The reference program's roundings to bfloat16 on the way count: a program that leaves them out, or rounds other values in their place, can miss the bound.
Values may be sent and summed in bfloat16 or wider, within the bound.
No kernel may reach another device: no remote copies, remote signals or barrier semaphores. Data moves between devices by JAX's collectives and lax.ppermute only.
A program may use at most 192 MiB of HBM per device.

```python
import math
import jax
import jax.numpy as jnp
import numpy as np
from jax import lax

D = 18432
FF = 36864
HEADS = 24
DH = 256
CACHE = 512
B = 64


def draw_k_cache(key, part):
    first = jax.random.fold_in(key, 0)
    base = jax.random.normal(first, (B, CACHE, DH), jnp.float32)
    return jnp.clip(base, -200.0, 200.0).astype(jnp.bfloat16)


def block_levels(own_key, dims, pieces, low, largest):
    def one(dim, shards_of):
        draws = jax.random.uniform(jax.random.fold_in(jax.random.fold_in(own_key, 6), dim), (shards_of,), jnp.float32, low / len(pieces), largest / len(pieces))
        return jnp.repeat(jnp.exp(draws), dims[dim] // shards_of).reshape((-1,) + (1,) * (len(dims) - dim - 1))

    loudness = one(*pieces[0])
    for cut in pieces[1:]:
        loudness = loudness * one(*cut)
    return loudness


def profile(number_of, total, bound, skew):
    portions = [(1 << 20) // math.isqrt(grade ** skew) + 1 for grade in range(2, number_of + 1)]
    rest, given = total - bound - (number_of - 1), [1] * (number_of - 1)
    while rest > 0:
        free = [i for i in range(number_of - 1) if given[i] < bound]
        whole, left = sum([portions[i] for i in free]), rest
        for i in free:
            extra = min(bound - given[i], max(1, left * portions[i] // whole), rest)
            given[i] = given[i] + extra
            rest = rest - extra
    return np.array([bound] + given)


def uneven(key, count, total, reach, slope):
    if count == 2:
        one = jax.random.randint(key, (), max(1, total - reach), min(reach, total - 1) + 1)
        return jnp.stack([one, total - one])
    tallies = jnp.asarray(profile(count, total, reach, slope), jnp.int32)
    couples = (count - 1) // 2
    donor, taker = tallies[1:1 + 2 * couples:2], tallies[2:2 + 2 * couples:2]
    room = jnp.minimum(donor - 1, reach - taker)
    shifted = jax.random.randint(jax.random.fold_in(key, 1), (couples,), 0, 1 << 20) % (room + 1)
    tallies = tallies.at[1:1 + 2 * couples:2].set(donor - shifted).at[2:2 + 2 * couples:2].set(taker + shifted)
    return tallies[jax.random.permutation(jax.random.fold_in(key, 2), count)]


def bell_draw(rng, extent, deviation, bound, shards=(), kind=jnp.bfloat16):
    gain = block_levels(rng, extent, shards, -0.22, 0.18) if shards else 1.0
    array = jax.random.normal(rng, extent, jnp.float32) * deviation * gain
    return jnp.minimum(jnp.maximum(array, -bound), bound).astype(kind)


def setup_inputs(seed: int = 0) -> dict:
    arg_keys = jax.random.split(jax.random.key(seed), 10)
    return {
        "stream": bell_draw(arg_keys[0], (B, D), 1.0, 6.0, ((0, 32),)),
        "norm_gain": jnp.clip(1.0 + 0.18 * jax.random.normal(arg_keys[1], (D,), jnp.float32), 0.1, 1.9),
        "w_gate": bell_draw(arg_keys[2], (D, FF), D ** -0.5, 0.046875, ((0, 8), (1, 4))),
        "w_up": bell_draw(arg_keys[3], (D, FF), D ** -0.5, 0.046875, ((0, 8), (1, 4))),
        "w_query": bell_draw(arg_keys[4], (D, HEADS * DH), D ** -0.5, 0.046875, ((0, 8), (1, 4))),
        "w_keyval": bell_draw(arg_keys[5], (D, 2 * DH), D ** -0.5, 0.046875, ((0, 8), (1, 4))),
        "k_cache": draw_k_cache(jax.random.fold_in(arg_keys[9], 71), 0),
        "v_cache": bell_draw(arg_keys[7], (B, CACHE, DH), 1.0, 6.0, ((0, 32),)),
        "lengths": uneven(arg_keys[8], B, B * CACHE // 2, CACHE, 2).astype(jnp.int32),
    }


def reference(stream, norm_gain, w_gate, w_up, w_query, w_keyval, k_cache, v_cache, lengths):
    values = stream.astype(jnp.float32)
    mean = lax.optimization_barrier(jnp.mean(values, axis=1, keepdims=True))
    centred = values - mean
    variance = lax.optimization_barrier(jnp.mean(centred * centred, axis=1, keepdims=True))
    normed = (centred / jnp.sqrt(variance + 1e-05) * norm_gain[None, :]).astype(jnp.bfloat16)
    gate = jnp.dot(normed, w_gate, preferred_element_type=jnp.float32)
    up_proj = jnp.dot(normed, w_up, preferred_element_type=jnp.float32)
    hidden = (jax.nn.silu(gate) * up_proj).astype(jnp.bfloat16)
    query = jnp.dot(normed, w_query, preferred_element_type=jnp.float32).astype(jnp.bfloat16)
    keyval = jnp.dot(normed, w_keyval, preferred_element_type=jnp.float32).astype(jnp.bfloat16)
    query = query.reshape(B, HEADS, DH).astype(jnp.float32)
    new_key = keyval[:, :DH].astype(jnp.float32)
    new_value = keyval[:, DH:].astype(jnp.float32)
    scale = DH ** (-0.5)
    scores = jnp.einsum('bhd,bld->bhl', query, k_cache.astype(jnp.float32)) * scale
    score_new = jnp.einsum('bhd,bd->bh', query, new_key) * scale
    mask = (jnp.arange(CACHE, dtype=jnp.int32)[None, :] < lengths[:, None])[:, None, :]
    top = jnp.maximum(lax.optimization_barrier(jnp.max(jnp.where(mask, scores, -1e+30), axis=2)), score_new)
    exponent = jnp.where(mask, jnp.exp(scores - top[:, :, None]), 0.0)
    exponent_new = jnp.exp(score_new - top)
    total = lax.optimization_barrier(jnp.sum(exponent, axis=2)) + exponent_new
    weights = (exponent / total[:, :, None]).astype(jnp.bfloat16).astype(jnp.float32)
    weights_new = (exponent_new / total).astype(jnp.bfloat16).astype(jnp.float32)
    context = jnp.einsum('bhl,bld->bhd', weights, v_cache.astype(jnp.float32))
    context = context + weights_new[:, :, None] * new_value[:, None, :]
    return (hidden, context.reshape(B, HEADS * DH).astype(jnp.bfloat16))
```

```python
import functools

import jax
import jax.numpy as jnp
from jax import lax
from jax.experimental import pallas as pl
from jax.experimental.pallas import tpu as pltpu
from jax.sharding import PartitionSpec as P

HEADS = 24
DH = 256
EPS = 1e-05
PORTIONS = (3, 5, 4)

BF16 = jnp.bfloat16
F32 = jnp.float32
VMEM = pl.BlockSpec(memory_space=pltpu.VMEM)
ANY = pl.BlockSpec(memory_space=pl.ANY)
SMEM = pl.BlockSpec(memory_space=pltpu.SMEM)


def shape(dims, dtype):
    return jax.ShapeDtypeStruct(tuple(dims), dtype)


def matmul(a, b):
    return jnp.dot(a, b, preferred_element_type=F32)


def swap(x, axis, bit):
    size = lax.axis_size(axis)
    return lax.ppermute(x, axis, [(i, i ^ bit) for i in range(size)])


def bits_of(size):
    return [1 << t for t in range(size.bit_length() - 1)]


def norm_kernel(blocks, where_ref, x_ref, gain_ref, keep_ref, send_ref):
    values = x_ref[...].astype(F32)
    width = values.shape[1]
    mean = jnp.sum(values, axis=1, keepdims=True) / width
    centred = values - mean
    variance = jnp.sum(centred * centred, axis=1, keepdims=True) / width
    root = jnp.sqrt(variance + EPS)
    part = width // blocks
    for k in range(blocks):
        start = pl.multiple_of((where_ref[0] ^ k) * part, 128)
        piece = x_ref[:, pl.ds(start, part)].astype(F32)
        normed = ((piece - mean) / root * gain_ref[:, pl.ds(start, part)]).astype(BF16)
        (send_ref if k % 2 else keep_ref)[k // 2] = normed


def normalise(stream, norm_gain, where, blocks):
    rows, width = stream.shape
    out = shape((blocks // 2, rows, width // blocks), BF16)
    return pl.pallas_call(
        functools.partial(norm_kernel, blocks),
        out_shape=(out, out),
        in_specs=[SMEM, VMEM, VMEM],
        out_specs=(VMEM, VMEM),
        cost_estimate=pl.CostEstimate(flops=20 * 10**9, bytes_accessed=10**6, transcendentals=0),
        compiler_params=pltpu.CompilerParams(vmem_limit_bytes=4 << 20),
        name="layer_norm",
    )(where, stream, norm_gain.reshape(1, width))


def attn_kernel(slots, order, where_ref, x_ref, wq_ref, wkv_ref, x_out, send_ref, keep_ref):
    total = x_ref.shape[0]
    groups = len(order)
    per = total // (groups * slots)
    row = lax.broadcasted_iota(jnp.int32, (total, total), 0)
    col = lax.broadcasted_iota(jnp.int32, (total, total), 1)
    base = (row // (per * groups)) * per + row % per
    slot = (row // per) % groups
    x = x_ref[...]

    def placed(want):
        source = jnp.zeros_like(row)
        for position, j in enumerate(order):
            source = jnp.where(want == j, position * (slots * per) + base, source)
        return matmul((col == source).astype(BF16), x).astype(BF16)

    x_out[...] = placed(slot ^ where_ref[1])
    relative = placed(slot)
    wide = wq_ref.shape[1]
    both = groups * per
    for lanes, w_ref in ((slice(0, wide), wq_ref), (slice(wide, wide + wkv_ref.shape[1]), wkv_ref)):
        part = matmul(relative, w_ref[...])
        for k in range(slots):
            (send_ref if k % 2 else keep_ref)[k // 2, :, lanes] = part[k * both : (k + 1) * both]


def attn_partials(x, w_query, w_keyval, where, slots, order):
    total, depth = x.shape
    cols = w_query.shape[1] + w_keyval.shape[1]
    out = shape((slots // 2, total // slots, cols), F32)
    return pl.pallas_call(
        functools.partial(attn_kernel, slots, order),
        out_shape=(shape(x.shape, BF16), out, out),
        in_specs=[SMEM, VMEM, VMEM, VMEM],
        out_specs=(VMEM, VMEM, VMEM),
        cost_estimate=pl.CostEstimate(
            flops=2 * total * depth * cols, bytes_accessed=2 * depth * cols, transcendentals=0
        ),
        compiler_params=pltpu.CompilerParams(vmem_limit_bytes=6 << 20),
        name="attn_partials",
    )(where, x, w_query, w_keyval)


def ffn_kernel(slots, first, count, x_ref, gate_ref, up_ref, send_ref, keep_ref, held, sems):
    tile = held.shape[2]
    rows = x_ref.shape[0] // slots

    def fetch(step, slot):
        columns = pl.ds(pl.multiple_of((first + step) * tile, tile), tile)
        return pltpu.make_async_copy(up_ref.at[:, columns], held.at[slot], sems.at[slot])

    for step in range(min(2, count)):
        fetch(step, step).start()

    def body(step, carry):
        slot = lax.rem(step, 2)
        x = x_ref[...]
        gate = matmul(x, gate_ref[:, pl.ds(pl.multiple_of((first + step) * tile, tile), tile)])
        fetch(step, slot).wait()
        up = matmul(x, held[slot])
        lanes = pl.ds(pl.multiple_of(step * tile, tile), tile)
        for k in range(slots):
            mine = slice(k * rows, (k + 1) * rows)
            both = jnp.concatenate([gate[mine], up[mine]], axis=0)
            ref = send_ref if k % 2 else keep_ref
            ref[k // 2, :, lanes] = both.astype(ref.dtype)

        @pl.when(step + 2 < count)
        def _():
            fetch(step + 2, slot).start()

        return carry

    lax.fori_loop(0, count, body, 0)


def ffn_partials(x, w_gate, w_up, slots, tile, first, count):
    total, depth = x.shape
    cols = count * tile
    dims = (slots // 2, 2 * total // slots, cols)
    return pl.pallas_call(
        functools.partial(ffn_kernel, slots, first, count),
        out_shape=(shape(dims, BF16), shape(dims, F32)),
        in_specs=[VMEM, VMEM, ANY],
        out_specs=(VMEM, VMEM),
        scratch_shapes=[pltpu.VMEM((2, depth, tile), BF16), pltpu.SemaphoreType.DMA((2,))],
        cost_estimate=pl.CostEstimate(
            flops=4 * total * depth * cols, bytes_accessed=2 * depth * cols, transcendentals=0
        ),
        compiler_params=pltpu.CompilerParams(vmem_limit_bytes=10 << 20),
        name="ffn_partials_%d" % first,
    )(x, w_gate, w_up)


def scatter_sum(send, keep, size, dtype):
    for bit in bits_of(size):
        keep = keep + swap(send, "gx", bit).astype(F32)
        if keep.shape[0] > 1:
            send, keep = keep[1::2].astype(dtype), keep[0::2]
    return keep[0]


def attention_kernel(order, where_ref, lengths_ref, pieces_ref, k_ref, v_ref, out_ref, q_ref):
    rows, cache, _ = k_ref.shape
    groups = len(order)
    keyval_cols = 2 * DH // groups
    query_cols = pieces_ref.shape[2] - keyval_cols
    per = query_cols // DH
    heads = groups * per
    scale = DH ** (-0.5)
    contexts = []
    for b in range(rows):
        halves = []
        for g in range(groups):
            slot = where_ref[1] ^ g
            position = jnp.int32(0)
            for p, j in enumerate(order):
                position = jnp.where(slot == j, p, position)
            piece = pieces_ref[position].astype(F32)[b : b + 1]
            for h in range(per):
                q_ref[g * per + h : g * per + h + 1] = piece[:, h * DH : (h + 1) * DH]
            halves.append(piece[:, query_cols:])
        keyval = jnp.concatenate(halves, axis=1)
        new_key, new_value = keyval[:, :DH], keyval[:, DH:]
        query = q_ref[...]
        scores = lax.dot_general(
            query.astype(BF16), k_ref[b], (((1,), (1,)), ((), ())), preferred_element_type=F32
        ) * scale
        score_new = jnp.sum(query * new_key, axis=1, keepdims=True) * scale
        mask = lax.broadcasted_iota(jnp.int32, (heads, cache), 1) < lengths_ref[b]
        top = jnp.maximum(jnp.max(jnp.where(mask, scores, -1e30), axis=1, keepdims=True), score_new)
        exponent = jnp.where(mask, jnp.exp(scores - top), 0.0)
        exponent_new = jnp.exp(score_new - top)
        total = jnp.sum(exponent, axis=1, keepdims=True) + exponent_new
        weights = (exponent / total).astype(BF16)
        weights_new = (exponent_new / total).astype(BF16).astype(F32)
        contexts.append(matmul(weights, v_ref[b]) + weights_new * new_value)
    for h in range(heads):
        both = jnp.concatenate([c[h : h + 1] for c in contexts], axis=0)
        out_ref[:, h * DH : (h + 1) * DH] = both.astype(BF16)


def attention(pieces, k_cache, v_cache, lengths, where, order):
    rows, cache, _ = k_cache.shape
    return pl.pallas_call(
        functools.partial(attention_kernel, order),
        out_shape=shape((rows, HEADS * DH), BF16),
        in_specs=[SMEM, SMEM, VMEM, VMEM, VMEM],
        out_specs=VMEM,
        scratch_shapes=[pltpu.VMEM((HEADS, DH), F32)],
        cost_estimate=pl.CostEstimate(
            flops=4 * rows * HEADS * cache * DH, bytes_accessed=4 * rows * cache * DH, transcendentals=0
        ),
        compiler_params=pltpu.CompilerParams(vmem_limit_bytes=6 << 20),
        name="attention",
    )(where, lengths, pieces, k_cache, v_cache)


def body(stream, norm_gain, w_gate, w_up, w_query, w_keyval, k_cache, v_cache, lengths):
    size, groups = lax.axis_size("gx"), lax.axis_size("gy")
    where = jnp.stack([lax.axis_index("gx"), lax.axis_index("gy")]).astype(jnp.int32)
    rows = stream.shape[0]
    depth, ff = w_gate.shape

    keep, send = normalise(stream, norm_gain, where, size)
    keep = keep[:, None]
    send = send[:, None]
    for bit in bits_of(size):
        keep = jnp.concatenate([keep, swap(send, "gx", bit)], axis=1)
        if keep.shape[0] > 1:
            send, keep = keep[1::2], keep[0::2]
    x = keep.reshape(size * rows, depth)
    order = [0]
    for bit in bits_of(groups)[::-1]:
        x = jnp.concatenate([x, swap(x, "gy", bit)], axis=0)
        order = order + [j ^ bit for j in order]

    x, send, keep = attn_partials(x, w_query, w_keyval, where, size, order)

    tile = max(t for t in range(128, 769, 128) if ff % t == 0)
    blocks = ff // tile
    edges = [round(blocks * sum(PORTIONS[:i]) / sum(PORTIONS)) for i in range(len(PORTIONS) + 1)]
    halves = []
    for first, last in zip(edges[:-1], edges[1:]):
        if last > first:
            halves.append(ffn_partials(x, w_gate, w_up, size, tile, first, last - first))

    projected = scatter_sum(send, keep, size, F32).astype(BF16)
    pieces = projected.reshape(groups, 1, rows, projected.shape[1])
    for bit in bits_of(groups)[::-1]:
        middle = pieces.shape[0] // 2
        pieces = jnp.concatenate([pieces[:middle], swap(pieces[middle:], "gy", bit)], axis=1)
    context = attention(pieces[0], k_cache, v_cache, lengths, where, order)

    hidden = []
    for send, keep in halves:
        both = scatter_sum(send, keep, size, BF16)
        middle = both.shape[0] // 2
        hidden.append((jax.nn.silu(both[:middle]) * both[middle:]).astype(BF16))
    return jnp.concatenate(hidden, axis=1), context


def solution(mesh):
    return jax.shard_map(
        body,
        mesh=mesh,
        in_specs=(
            P(("gx", "gy"), None),
            P(),
            P("gx", "gy"),
            P("gx", "gy"),
            P("gx", "gy"),
            P("gx", "gy"),
            P(("gx", "gy"), None, None),
            P(("gx", "gy"), None, None),
            P(("gx", "gy")),
        ),
        out_specs=(P("gx", "gy"), P(("gx", "gy"), None)),
        check_vma=False,
    )
```

```python
import functools

import jax
import jax.numpy as jnp
from jax import lax
from jax.experimental import pallas as pl
from jax.experimental.pallas import tpu as pltpu
from jax.sharding import PartitionSpec as P

HEADS = 24
DH = 256
EPS = 1e-05
PORTIONS = ((1, 4), (5,), (2,))
TILE = 768
AHEAD = 1
SLOTS = 3

BF16 = jnp.bfloat16
F32 = jnp.float32
VMEM = pl.BlockSpec(memory_space=pltpu.VMEM)
HBM = pl.BlockSpec(memory_space=pltpu.HBM)
ANY = pl.BlockSpec(memory_space=pl.ANY)
SMEM = pl.BlockSpec(memory_space=pltpu.SMEM)


def shape(dims, dtype):
    return jax.ShapeDtypeStruct(tuple(dims), dtype)


def matmul(a, b):
    return jnp.dot(a, b, preferred_element_type=F32)


def in_hbm(x):
    return pltpu.with_memory_space_constraint(x, pltpu.HBM)


def in_vmem(x):
    return pltpu.with_memory_space_constraint(x, pltpu.VMEM)


def swap(x, axis, bit):
    size = lax.axis_size(axis)
    return lax.ppermute(x, axis, [(i, i ^ bit) for i in range(size)])


def bits_of(size):
    return [1 << t for t in range(size.bit_length() - 1)]


def norm_kernel(blocks, x_hbm, gain_hbm, keep_ref, send_ref, x_ref, gain_ref, sems):
    copies = [
        pltpu.make_async_copy(source, target, sems.at[i])
        for i, (source, target) in enumerate(((x_hbm, x_ref), (gain_hbm, gain_ref)))
    ]
    for copy in copies:
        copy.start()
    copies[0].wait()
    values = x_ref[...].astype(F32)
    width = values.shape[1]
    mean = jnp.sum(values, axis=1, keepdims=True) / width
    centred = values - mean
    variance = jnp.sum(centred * centred, axis=1, keepdims=True) / width
    root = jnp.sqrt(variance + EPS)
    part = width // blocks
    copies[1].wait()
    for k in range(blocks):
        start = pl.multiple_of((lax.axis_index("gx") ^ k) * part, 128)
        piece = x_ref[:, pl.ds(start, part)].astype(F32)
        normed = ((piece - mean) / root * gain_ref[:, pl.ds(start, part)]).astype(BF16)
        (send_ref if k % 2 else keep_ref)[k // 2, 0] = normed


def normalise(stream, norm_gain, blocks):
    rows, width = stream.shape
    out = shape((blocks // 2, 1, rows, width // blocks), BF16)
    return pl.pallas_call(
        functools.partial(norm_kernel, blocks),
        out_shape=(out, out),
        in_specs=[HBM, HBM],
        out_specs=(VMEM, VMEM),
        scratch_shapes=[
            pltpu.VMEM((rows, width), BF16),
            pltpu.VMEM((1, width), F32),
            pltpu.SemaphoreType.DMA((2,)),
        ],
        cost_estimate=pl.CostEstimate(flops=20 * 10**9, bytes_accessed=10**6, transcendentals=0),
        compiler_params=pltpu.CompilerParams(vmem_limit_bytes=2 << 20),
        name="layer_norm",
    )(in_hbm(stream), in_hbm(norm_gain.reshape(1, width)))


def join_kernel(sent, keep_ref, arrived_ref, *outs):
    slots, count = keep_ref.shape[:2]
    if slots == 1:
        pieces = [ref[0, i].astype(F32) for ref in (keep_ref, arrived_ref) for i in range(count)]
        outs[0][...] = jnp.concatenate(pieces, axis=0).astype(BF16)
        return
    send_out, keep_out = outs
    places = [0, 0]
    for s in range(slots):
        way = s in sent
        out = send_out if way else keep_out
        for i in range(count):
            out[places[way], i] = keep_ref[s, i]
            out[places[way], count + i] = arrived_ref[s, i]
        places[way] += 1


def join(keep, arrived, sent):
    slots, count, rows, cols = keep.shape
    if slots == 1:
        out_shape = (shape((2 * count * rows, cols), BF16),)
    else:
        out_shape = (shape((slots // 2, 2 * count, rows, cols), BF16),) * 2
    return pl.pallas_call(
        functools.partial(join_kernel, tuple(sent)),
        out_shape=out_shape,
        in_specs=[VMEM, VMEM],
        out_specs=(VMEM,) * len(out_shape),
        compiler_params=pltpu.CompilerParams(vmem_limit_bytes=2 << 20),
        name="join_%d_%d" % (slots, cols),
    )(keep, arrived)


def split(value):
    high = value.astype(BF16).astype(F32)
    return jnp.concatenate([high, value - high], axis=0).astype(BF16)


def heads_part(slots, order, x_ref, wq_ref, wkv_ref, x_out, send_ref, keep_ref):
    total = x_ref.shape[0]
    groups = len(order)
    per = total // (groups * slots)
    row = lax.broadcasted_iota(jnp.int32, (total, total), 0)
    col = lax.broadcasted_iota(jnp.int32, (total, total), 1)
    base = (row // (per * groups)) * per + row % per
    slot = (row // per) % groups
    x = x_ref[...]

    def placed(want):
        source = jnp.zeros_like(row)
        for position, j in enumerate(order):
            source = jnp.where(want == j, position * (slots * per) + base, source)
        return matmul((col == source).astype(BF16), x).astype(BF16)

    x_out[...] = placed(slot ^ lax.axis_index("gy"))
    relative = placed(slot)
    both = groups * per
    at = 0
    for w_ref in (wq_ref, wkv_ref):
        lanes = slice(at, at + w_ref.shape[1])
        part = matmul(relative, w_ref[...])
        for k in range(slots):
            mine = part[k * both : (k + 1) * both]
            if k % 2:
                send_ref[k // 2, :, lanes] = split(mine)
            else:
                keep_ref[k // 2, :, lanes] = jnp.concatenate([mine, jnp.zeros_like(mine)], axis=0)
        at += w_ref.shape[1]
    return at


def fetch_kernel(first, w_ref, after_ref, out_ref, sem):
    copy = pltpu.make_async_copy(w_ref.at[:, pl.ds(first, out_ref.shape[1])], out_ref, sem)
    copy.start()
    copy.wait()


def fetch(weights, first, cols, after):
    depth = weights.shape[0]
    return pl.pallas_call(
        functools.partial(fetch_kernel, first),
        out_shape=pltpu.VMEM((depth, cols), BF16),
        in_specs=[HBM, ANY],
        out_specs=VMEM,
        scratch_shapes=[pltpu.SemaphoreType.DMA],
        cost_estimate=pl.CostEstimate(flops=0, bytes_accessed=2 * depth * cols, transcendentals=0),
        compiler_params=pltpu.CompilerParams(vmem_limit_bytes=1 << 20),
        name="fetch_%d" % first,
    )(in_hbm(weights), after)


def partials_kernel(slots, first, count, tile, ready, order, *refs):
    x_ref, gate_ref, up_ref = refs[:3]
    resident = []
    for piece in refs[3 : 3 + ready]:
        resident += [piece.at[:, pl.ds(i * tile, tile)] for i in range(piece.shape[1] // tile)]
    held, gates, sems = refs[-3:]
    rest = refs[3 + ready : -3]
    rows = x_ref.shape[0] // slots
    room = held.shape[0]
    sources = []
    for step in range(count):
        columns = pl.ds((first + step) * tile, tile)
        if step >= len(resident):
            sources.append(gate_ref.at[:, columns])
        sources.append(up_ref.at[:, columns])
    copies = [pltpu.make_async_copy(source, held.at[i % room], sems.at[i % room]) for i, source in enumerate(sources)]
    for copy in copies[:room]:
        copy.start()
    if order is None:
        send_ref, keep_ref = rest[-2:]
        base = 0
        x = x_ref[...]
    else:
        wq_ref, wkv_ref = rest[:2]
        x_out, send_ref, keep_ref = rest[-3:]
        base = heads_part(slots, order, x_ref, wq_ref, wkv_ref, x_out, send_ref, keep_ref)
        x = x_out[...]
    at = 0

    def from_stream():
        nonlocal at
        copies[at].wait()
        out = matmul(x, held[at % room])
        if at + room < len(copies):
            copies[at + room].start()
        at += 1
        return out

    if resident:
        gates[0] = matmul(x, resident[0][...])
    for step in range(count):
        if step + 1 < len(resident):
            gates[(step + 1) % 2] = matmul(x, resident[step + 1][...])
        gate = gates[step % 2] if step < len(resident) else from_stream()
        up = from_stream()
        lanes = slice(base + step * tile, base + (step + 1) * tile)
        for k in range(slots):
            mine = slice(k * rows, (k + 1) * rows)
            both = jnp.concatenate([gate[mine], up[mine]], axis=0)
            ref = send_ref if k % 2 else keep_ref
            ref[k // 2, :, lanes] = both.astype(ref.dtype)


def partials(x, w_gate, w_up, pieces, slots, tile, first, count, heads=(), order=None, after=()):
    total, depth = x.shape
    cols = count * tile + sum(w.shape[1] for w in heads)
    out_shape = [shape(x.shape, BF16)] if heads else []
    dims = (slots // 2, 2 * total // slots, cols)
    out_shape += [shape(dims, BF16), shape(dims, F32)]
    room = max(1, min(SLOTS, 2 * count - sum(p.shape[1] for p in pieces) // tile))
    return pl.pallas_call(
        functools.partial(partials_kernel, slots, first, count, tile, len(pieces), order),
        out_shape=tuple(out_shape),
        in_specs=[VMEM, HBM, HBM] + [VMEM] * (len(pieces) + len(heads)) + [ANY] * len(after),
        out_specs=(VMEM,) * len(out_shape),
        scratch_shapes=[
            pltpu.VMEM((room, depth, tile), BF16),
            pltpu.VMEM((2, total, tile), F32),
            pltpu.SemaphoreType.DMA((room,)),
        ],
        cost_estimate=pl.CostEstimate(
            flops=4 * total * depth * cols, bytes_accessed=4 * depth * cols, transcendentals=0
        ),
        compiler_params=pltpu.CompilerParams(vmem_limit_bytes=2 * room * depth * tile + (3 << 20)),
        name="partials_%d" % first,
    )(x, in_hbm(w_gate), in_hbm(w_up), *[in_vmem(w) for w in (*pieces, *heads)], *after)


def combine_kernel(wide, count, *refs):
    send_ref, keep_ref = refs[-2:]
    at = 0
    for keep, arrived in zip(refs[: 2 * count : 2], refs[1 : 2 * count : 2]):
        for s in range(keep.shape[0]):
            both = keep[s] + arrived[s].astype(F32)
            lanes = slice(at, at + keep.shape[2])
            if s % 2 == 0:
                keep_ref[s // 2, :, lanes] = both
                continue
            send_ref[s // 2, :, lanes] = both.astype(BF16)
            if at == 0 and wide:
                rows = both.shape[0] // 2
                send_ref[s // 2, :, :wide] = split(both[:rows, :wide] + both[rows:, :wide])
        at += keep.shape[2]


def combine(parts, wide, after=()):
    slots, rows, _ = parts[0][0].shape
    cols = sum(keep.shape[2] for keep, _ in parts)
    dims = (slots // 2, rows, cols)
    return pl.pallas_call(
        functools.partial(combine_kernel, wide, len(parts)),
        out_shape=(shape(dims, BF16), shape(dims, F32)),
        in_specs=[VMEM] * (2 * len(parts)) + [ANY] * len(after),
        out_specs=(VMEM, VMEM),
        compiler_params=pltpu.CompilerParams(vmem_limit_bytes=2 << 20),
        name="combine_%d" % cols,
    )(*[a for part in parts for a in part], *after)


def finish_kernel(wide, keep_ref, arrived_ref, *refs):
    both = keep_ref[0] + arrived_ref[0].astype(F32)
    rows = both.shape[0] // 2
    if wide:
        earlier, (send_ref, own_ref, hidden_ref) = refs[:-3], refs[-3:]
        middle, _, per, _ = own_ref.shape
        heads = both[:rows, :wide] + both[rows:, :wide]
        for j in range(2 * middle):
            piece = heads[j * per : (j + 1) * per].astype(BF16)
            (own_ref if j < middle else send_ref)[j % middle, 0] = piece
    else:
        earlier, hidden_ref = refs[:-1], refs[-1]
    at = 0
    for ref in earlier:
        hidden_ref[:, at : at + ref.shape[1]] = ref[...]
        at += ref.shape[1]
    gate, up = both[:rows, wide:], both[rows:, wide:]
    hidden_ref[:, at:] = (gate * (1.0 / (1.0 + jnp.exp(-gate))) * up).astype(BF16)


def finish(keep, arrived, wide, groups, earlier):
    _, rows, cols = keep.shape
    out = [shape((rows // 2, cols - wide + sum(e.shape[1] for e in earlier)), BF16)]
    if wide:
        out = [shape((groups // 2, 1, rows // 2 // groups, wide), BF16)] * 2 + out
    return pl.pallas_call(
        functools.partial(finish_kernel, wide),
        out_shape=tuple(out),
        in_specs=[VMEM] * (2 + len(earlier)),
        out_specs=(VMEM,) * len(out),
        compiler_params=pltpu.CompilerParams(vmem_limit_bytes=4 << 20),
        name="finish_%d" % cols,
    )(keep, arrived, *earlier)


def attention_kernel(order, lengths_ref, own_ref, arrived_ref, k_ref, v_ref, out_ref, q_ref, pieces_ref):
    rows, cache, _ = k_ref.shape
    groups = len(order)
    keyval_cols = 2 * DH // groups
    query_cols = own_ref.shape[3] - keyval_cols
    per = query_cols // DH
    heads = groups * per
    scale = DH ** (-0.5)
    for i in range(groups // 2):
        pieces_ref[i] = own_ref[0, i].astype(F32)
        pieces_ref[groups // 2 + i] = arrived_ref[0, i].astype(F32)
    contexts = []
    for b in range(rows):
        halves = []
        for g in range(groups):
            slot = lax.axis_index("gy") ^ g
            position = jnp.int32(0)
            for p, j in enumerate(order):
                position = jnp.where(slot == j, p, position)
            piece = pieces_ref[position][b : b + 1]
            for h in range(per):
                q_ref[g * per + h : g * per + h + 1] = piece[:, h * DH : (h + 1) * DH]
            halves.append(piece[:, query_cols:])
        keyval = jnp.concatenate(halves, axis=1)
        new_key, new_value = keyval[:, :DH], keyval[:, DH:]
        query = q_ref[...]
        scores = lax.dot_general(
            query.astype(BF16), k_ref[b], (((1,), (1,)), ((), ())), preferred_element_type=F32
        ) * scale
        score_new = jnp.sum(query * new_key, axis=1, keepdims=True) * scale
        mask = lax.broadcasted_iota(jnp.int32, (heads, cache), 1) < lengths_ref[b]
        top = jnp.maximum(jnp.max(jnp.where(mask, scores, -1e30), axis=1, keepdims=True), score_new)
        exponent = jnp.where(mask, jnp.exp(scores - top), 0.0)
        exponent_new = jnp.exp(score_new - top)
        total = jnp.sum(exponent, axis=1, keepdims=True) + exponent_new
        weights = (exponent / total).astype(BF16)
        weights_new = (exponent_new / total).astype(BF16).astype(F32)
        contexts.append(matmul(weights, v_ref[b]) + weights_new * new_value)
    for h in range(heads):
        both = jnp.concatenate([c[h : h + 1] for c in contexts], axis=0)
        out_ref[:, h * DH : (h + 1) * DH] = both.astype(BF16)


def attention(own, arrived, k_cache, v_cache, lengths, order):
    rows, cache, _ = k_cache.shape
    return pl.pallas_call(
        functools.partial(attention_kernel, order),
        out_shape=shape((rows, HEADS * DH), BF16),
        in_specs=[SMEM, VMEM, VMEM, VMEM, VMEM],
        out_specs=VMEM,
        scratch_shapes=[pltpu.VMEM((HEADS, DH), F32), pltpu.VMEM((len(order), rows, own.shape[3]), F32)],
        cost_estimate=pl.CostEstimate(
            flops=4 * rows * HEADS * cache * DH, bytes_accessed=4 * rows * cache * DH, transcendentals=0
        ),
        compiler_params=pltpu.CompilerParams(vmem_limit_bytes=6 << 20),
        name="attention",
    )(lengths, own, arrived, k_cache, v_cache)


def body(stream, norm_gain, w_gate, w_up, w_query, w_keyval, k_cache, v_cache, lengths):
    size, groups = lax.axis_size("gx"), lax.axis_size("gy")
    ff = w_gate.shape[1]
    wide = w_query.shape[1] + w_keyval.shape[1]
    tile = max(t for t in range(128, TILE + 1, 128) if ff % t == 0)
    blocks = ff // tile
    flat = [p for group in PORTIONS for p in group]
    edges = [round(blocks * sum(flat[:i]) / sum(flat)) for i in range(len(flat) + 1)]

    pieces = [[] for _ in flat]

    def swap_and_fetch(send, keep, axis, bit):
        arrived = swap(send, axis, bit)
        taken = [sum(p.shape[1] for p in held) // tile for held in pieces]
        left = [edges[i + 1] - edges[i] - taken[i] for i in range(len(flat))]
        portion = max(range(len(flat)), key=lambda i: left[i])
        count = min(AHEAD, left[portion])
        if count:
            piece = fetch(w_gate, (edges[portion] + taken[portion]) * tile, count * tile, send)
            piece, keep = lax.optimization_barrier((piece, keep))
            pieces[portion].append(piece)
        return keep, arrived

    bits = bits_of(size)
    keep, send = normalise(stream, norm_gain, size)
    for bit in bits[:-1]:
        keep, arrived = swap_and_fetch(send, keep, "gx", bit)
        send, keep = join(keep, arrived, range(1, keep.shape[0], 2))
    keep, arrived = swap_and_fetch(send, keep, "gx", bits[-1])
    (x,) = join(keep, arrived, ())
    order = [0]
    for bit in bits_of(groups)[::-1]:
        keep, arrived = swap_and_fetch(x, x, "gy", bit)
        x = jnp.concatenate([keep, arrived], axis=0)
        order = order + [j ^ bit for j in order]

    parts = []
    for i in range(len(flat)):
        first, count = edges[i], edges[i + 1] - edges[i]
        if i == 0:
            heads = (w_query, w_keyval)
            x, send, keep = partials(x, w_gate, w_up, pieces[i], size, tile, first, count, heads, tuple(order))
        else:
            after = (parts[i - 2][1],) if i > 1 else ()
            send, keep = partials(x, w_gate, w_up, pieces[i], size, tile, first, count, after=after)
        parts.append((keep, swap(send, "gx", bits[0])))

    hidden = []
    context = None
    at = 0
    for number, group in enumerate(PORTIONS):
        columns = 0 if number else wide
        here = parts[at : at + len(group)]
        at += len(group)
        after = (parts[at][0],) if at < len(flat) else ()
        for bit in bits[1:]:
            send, keep = combine(here, columns, after)
            after = ()
            here = [(keep, swap(send, "gx", bit))]
        *heads, part = finish(*here[0], columns, groups, hidden if at == len(flat) else [])
        hidden.append(part)
        if number:
            continue
        send, keep = heads
        for bit in bits_of(groups)[:0:-1]:
            send, keep = join(keep, swap(send, "gy", bit), range(keep.shape[0] // 2, keep.shape[0]))
        context = attention(keep, swap(send, "gy", 1), k_cache, v_cache, lengths, tuple(order))
    return hidden[-1], context


def solution(mesh):
    return jax.shard_map(
        body,
        mesh=mesh,
        in_specs=(
            P(("gx", "gy"), None),
            P(),
            P("gx", "gy"),
            P("gx", "gy"),
            P("gx", "gy"),
            P("gx", "gy"),
            P(("gx", "gy"), None, None),
            P(("gx", "gy"), None, None),
            P(("gx", "gy")),
        ),
        out_specs=(P("gx", "gy"), P(("gx", "gy"), None)),
        check_vma=False,
    )
```

```python
import functools

import jax
import jax.numpy as jnp
from jax import lax
from jax.experimental import pallas as pl
from jax.experimental.pallas import tpu as pltpu
from jax.sharding import PartitionSpec as P

HEADS = 24
DH = 256
EPS = 1e-05
PORTIONS = ((1,), (4,), (4,), (3,))
ORDER = (
    "K0", "K1", "S0", "K2", "S0", "S1", "K3", "S2", "F0", "S1", "J", "S3", "S2", "A", "S3", "F1",
    "F2", "F3",
)
TILE = 768
AHEAD = 2
SLOTS = 3
WEIGHT = 2 * 10**9

BF16 = jnp.bfloat16
F32 = jnp.float32
VMEM = pl.BlockSpec(memory_space=pltpu.VMEM)
HBM = pl.BlockSpec(memory_space=pltpu.HBM)
ANY = pl.BlockSpec(memory_space=pl.ANY)
SMEM = pl.BlockSpec(memory_space=pltpu.SMEM)


def shape(dims, dtype):
    return jax.ShapeDtypeStruct(tuple(dims), dtype)


def matmul(a, b):
    return jnp.dot(a, b, preferred_element_type=F32)


def in_hbm(x):
    return pltpu.with_memory_space_constraint(x, pltpu.HBM)


def in_vmem(x):
    return pltpu.with_memory_space_constraint(x, pltpu.VMEM)


def swap(x, axis, bit):
    size = lax.axis_size(axis)
    return lax.ppermute(x, axis, [(i, i ^ bit) for i in range(size)])


def bits_of(size):
    return [1 << t for t in range(size.bit_length() - 1)]


def norm_kernel(blocks, x_hbm, gain_hbm, keep_ref, send_ref, x_ref, gain_ref, sems):
    copies = [
        pltpu.make_async_copy(source, target, sems.at[i])
        for i, (source, target) in enumerate(((x_hbm, x_ref), (gain_hbm, gain_ref)))
    ]
    for copy in copies:
        copy.start()
    copies[0].wait()
    values = x_ref[...].astype(F32)
    width = values.shape[1]
    mean = jnp.sum(values, axis=1, keepdims=True) / width
    centred = values - mean
    variance = jnp.sum(centred * centred, axis=1, keepdims=True) / width
    root = jnp.sqrt(variance + EPS)
    part = width // blocks
    copies[1].wait()
    for k in range(blocks):
        start = pl.multiple_of((lax.axis_index("gx") ^ k) * part, 128)
        piece = x_ref[:, pl.ds(start, part)].astype(F32)
        normed = ((piece - mean) / root * gain_ref[:, pl.ds(start, part)]).astype(BF16)
        (send_ref if k % 2 else keep_ref)[k // 2, 0] = normed


def normalise(stream, norm_gain, blocks):
    rows, width = stream.shape
    out = shape((blocks // 2, 1, rows, width // blocks), BF16)
    return pl.pallas_call(
        functools.partial(norm_kernel, blocks),
        out_shape=(out, out),
        in_specs=[HBM, HBM],
        out_specs=(VMEM, VMEM),
        scratch_shapes=[
            pltpu.VMEM((rows, width), BF16),
            pltpu.VMEM((1, width), F32),
            pltpu.SemaphoreType.DMA((2,)),
        ],
        cost_estimate=pl.CostEstimate(flops=20 * 10**9, bytes_accessed=10**6, transcendentals=0),
        compiler_params=pltpu.CompilerParams(vmem_limit_bytes=2 << 20),
        name="layer_norm",
    )(in_hbm(stream), in_hbm(norm_gain.reshape(1, width)))


def join_kernel(sent, keep_ref, arrived_ref, *refs):
    slots, count = keep_ref.shape[:2]
    outs = refs[-1:] if slots == 1 else refs[-2:]
    if slots == 1:
        pieces = [ref[0, i].astype(F32) for ref in (keep_ref, arrived_ref) for i in range(count)]
        outs[0][...] = jnp.concatenate(pieces, axis=0).astype(BF16)
        return
    send_out, keep_out = outs
    places = [0, 0]
    for s in range(slots):
        way = s in sent
        out = send_out if way else keep_out
        for i in range(count):
            out[places[way], i] = keep_ref[s, i]
            out[places[way], count + i] = arrived_ref[s, i]
        places[way] += 1


def join(keep, arrived, sent, after=()):
    slots, count, rows, cols = keep.shape
    if slots == 1:
        out_shape = (shape((2 * count * rows, cols), BF16),)
    else:
        out_shape = (shape((slots // 2, 2 * count, rows, cols), BF16),) * 2
    return pl.pallas_call(
        functools.partial(join_kernel, tuple(sent)),
        out_shape=out_shape,
        in_specs=[VMEM, VMEM] + [ANY] * len(after),
        out_specs=(VMEM,) * len(out_shape),
        compiler_params=pltpu.CompilerParams(vmem_limit_bytes=2 << 20),
        cost_estimate=pl.CostEstimate(flops=WEIGHT, bytes_accessed=10**6, transcendentals=0),
        name="join_%d_%d" % (slots, cols),
    )(keep, arrived, *after)


def split(value):
    high = value.astype(BF16).astype(F32)
    return jnp.concatenate([high, value - high], axis=0).astype(BF16)


def heads_part(slots, order, x_ref, wq_ref, wkv_ref, x_out, send_ref, keep_ref):
    total = x_ref.shape[0]
    groups = len(order)
    per = total // (groups * slots)
    row = lax.broadcasted_iota(jnp.int32, (total, total), 0)
    col = lax.broadcasted_iota(jnp.int32, (total, total), 1)
    base = (row // (per * groups)) * per + row % per
    slot = (row // per) % groups
    x = x_ref[...]

    def placed(want):
        source = jnp.zeros_like(row)
        for position, j in enumerate(order):
            source = jnp.where(want == j, position * (slots * per) + base, source)
        return matmul((col == source).astype(BF16), x).astype(BF16)

    x_out[...] = placed(slot ^ lax.axis_index("gy"))
    relative = placed(slot)
    both = groups * per
    at = 0
    for w_ref in (wq_ref, wkv_ref):
        lanes = slice(at, at + w_ref.shape[1])
        part = matmul(relative, w_ref[...])
        for k in range(slots):
            mine = part[k * both : (k + 1) * both]
            if k % 2:
                send_ref[k // 2, :, lanes] = split(mine)
            else:
                keep_ref[k // 2, :, lanes] = jnp.concatenate([mine, jnp.zeros_like(mine)], axis=0)
        at += w_ref.shape[1]
    return at


def fetch_kernel(first, w_ref, after_ref, out_ref, sem):
    copy = pltpu.make_async_copy(w_ref.at[:, pl.ds(first, out_ref.shape[1])], out_ref, sem)
    copy.start()
    copy.wait()


def fetch(weights, first, cols, after):
    depth = weights.shape[0]
    return pl.pallas_call(
        functools.partial(fetch_kernel, first),
        out_shape=pltpu.VMEM((depth, cols), BF16),
        in_specs=[HBM, ANY],
        out_specs=VMEM,
        scratch_shapes=[pltpu.SemaphoreType.DMA],
        cost_estimate=pl.CostEstimate(flops=0, bytes_accessed=2 * depth * cols, transcendentals=0),
        compiler_params=pltpu.CompilerParams(vmem_limit_bytes=1 << 20),
        name="fetch_%d" % first,
    )(in_hbm(weights), after)


def partials_kernel(slots, first, count, tile, ready, order, *refs):
    x_ref, gate_ref, up_ref = refs[:3]
    resident = []
    for piece in refs[3 : 3 + ready]:
        resident += [piece.at[:, pl.ds(i * tile, tile)] for i in range(piece.shape[1] // tile)]
    held, gates, sems = refs[-3:]
    rest = refs[3 + ready : -3]
    rows = x_ref.shape[0] // slots
    room = held.shape[0]
    sources = []
    for step in range(count):
        columns = pl.ds((first + step) * tile, tile)
        if step >= len(resident):
            sources.append(gate_ref.at[:, columns])
        sources.append(up_ref.at[:, columns])
    copies = [pltpu.make_async_copy(source, held.at[i % room], sems.at[i % room]) for i, source in enumerate(sources)]
    for copy in copies[:room]:
        copy.start()
    if order is None:
        send_ref, keep_ref = rest[-2:]
        base = 0
        x = x_ref[...]
    else:
        wq_ref, wkv_ref = rest[:2]
        x_out, send_ref, keep_ref = rest[-3:]
        base = heads_part(slots, order, x_ref, wq_ref, wkv_ref, x_out, send_ref, keep_ref)
        x = x_out[...]
    at = 0

    def from_stream():
        nonlocal at
        copies[at].wait()
        out = matmul(x, held[at % room])
        if at + room < len(copies):
            copies[at + room].start()
        at += 1
        return out

    if resident:
        gates[0] = matmul(x, resident[0][...])
    for step in range(count):
        if step + 1 < len(resident):
            gates[(step + 1) % 2] = matmul(x, resident[step + 1][...])
        gate = gates[step % 2] if step < len(resident) else from_stream()
        up = from_stream()
        lanes = slice(base + step * tile, base + (step + 1) * tile)
        for k in range(slots):
            mine = slice(k * rows, (k + 1) * rows)
            both = jnp.concatenate([gate[mine], up[mine]], axis=0)
            ref = send_ref if k % 2 else keep_ref
            ref[k // 2, :, lanes] = both.astype(ref.dtype)


def partials(x, w_gate, w_up, pieces, slots, tile, first, count, heads=(), order=None, after=()):
    total, depth = x.shape
    cols = count * tile + sum(w.shape[1] for w in heads)
    out_shape = [shape(x.shape, BF16)] if heads else []
    dims = (slots // 2, 2 * total // slots, cols)
    out_shape += [shape(dims, BF16), shape(dims, F32)]
    room = max(1, min(SLOTS, 2 * count - sum(p.shape[1] for p in pieces) // tile))
    return pl.pallas_call(
        functools.partial(partials_kernel, slots, first, count, tile, len(pieces), order),
        out_shape=tuple(out_shape),
        in_specs=[VMEM, HBM, HBM] + [VMEM] * (len(pieces) + len(heads)) + [ANY] * len(after),
        out_specs=(VMEM,) * len(out_shape),
        scratch_shapes=[
            pltpu.VMEM((room, depth, tile), BF16),
            pltpu.VMEM((2, total, tile), F32),
            pltpu.SemaphoreType.DMA((room,)),
        ],
        cost_estimate=pl.CostEstimate(
            flops=4 * total * depth * cols, bytes_accessed=4 * depth * cols, transcendentals=0
        ),
        compiler_params=pltpu.CompilerParams(vmem_limit_bytes=2 * room * depth * tile + (3 << 20)),
        name="partials_%d" % first,
    )(x, in_hbm(w_gate), in_hbm(w_up), *[in_vmem(w) for w in (*pieces, *heads)], *after)


def combine_kernel(wide, count, *refs):
    send_ref, keep_ref = refs[-2:]
    at = 0
    for keep, arrived in zip(refs[: 2 * count : 2], refs[1 : 2 * count : 2]):
        for s in range(keep.shape[0]):
            both = keep[s] + arrived[s].astype(F32)
            lanes = slice(at, at + keep.shape[2])
            if s % 2 == 0:
                keep_ref[s // 2, :, lanes] = both
                continue
            send_ref[s // 2, :, lanes] = both.astype(BF16)
            if at == 0 and wide:
                rows = both.shape[0] // 2
                send_ref[s // 2, :, :wide] = split(both[:rows, :wide] + both[rows:, :wide])
        at += keep.shape[2]


def combine(parts, wide, after=()):
    slots, rows, _ = parts[0][0].shape
    cols = sum(keep.shape[2] for keep, _ in parts)
    dims = (slots // 2, rows, cols)
    return pl.pallas_call(
        functools.partial(combine_kernel, wide, len(parts)),
        out_shape=(shape(dims, BF16), shape(dims, F32)),
        in_specs=[VMEM] * (2 * len(parts)) + [ANY] * len(after),
        out_specs=(VMEM, VMEM),
        compiler_params=pltpu.CompilerParams(vmem_limit_bytes=2 << 20),
        cost_estimate=pl.CostEstimate(flops=WEIGHT, bytes_accessed=10**6, transcendentals=0),
        name="combine_%d" % cols,
    )(*[a for part in parts for a in part], *after)


def finish_kernel(wide, ready, keep_ref, arrived_ref, *refs):
    both = keep_ref[0] + arrived_ref[0].astype(F32)
    rows = both.shape[0] // 2
    if wide:
        send_ref, own_ref, hidden_ref = refs[-3:]
        middle, _, per, _ = own_ref.shape
        heads = both[:rows, :wide] + both[rows:, :wide]
        for j in range(2 * middle):
            piece = heads[j * per : (j + 1) * per].astype(BF16)
            (own_ref if j < middle else send_ref)[j % middle, 0] = piece
    else:
        hidden_ref = refs[-1]
    at = 0
    for ref in refs[:ready]:
        hidden_ref[:, at : at + ref.shape[1]] = ref[...]
        at += ref.shape[1]
    gate, up = both[:rows, wide:], both[rows:, wide:]
    hidden_ref[:, at:] = (gate * (1.0 / (1.0 + jnp.exp(-gate))) * up).astype(BF16)


def finish(keep, arrived, wide, groups, earlier, after=()):
    _, rows, cols = keep.shape
    out = [shape((rows // 2, cols - wide + sum(e.shape[1] for e in earlier)), BF16)]
    if wide:
        out = [shape((groups // 2, 1, rows // 2 // groups, wide), BF16)] * 2 + out
    return pl.pallas_call(
        functools.partial(finish_kernel, wide, len(earlier)),
        out_shape=tuple(out),
        in_specs=[VMEM] * (2 + len(earlier)) + [ANY] * len(after),
        out_specs=(VMEM,) * len(out),
        compiler_params=pltpu.CompilerParams(vmem_limit_bytes=4 << 20),
        cost_estimate=pl.CostEstimate(flops=WEIGHT, bytes_accessed=10**6, transcendentals=0),
        name="finish_%d" % cols,
    )(keep, arrived, *earlier, *after)


def attention_kernel(order, lengths_ref, own_ref, arrived_ref, k_ref, v_ref, *refs):
    out_ref, q_ref, pieces_ref = refs[-3:]
    rows, cache, _ = k_ref.shape
    groups = len(order)
    keyval_cols = 2 * DH // groups
    query_cols = own_ref.shape[3] - keyval_cols
    per = query_cols // DH
    heads = groups * per
    scale = DH ** (-0.5)
    for i in range(groups // 2):
        pieces_ref[i] = own_ref[0, i].astype(F32)
        pieces_ref[groups // 2 + i] = arrived_ref[0, i].astype(F32)
    contexts = []
    for b in range(rows):
        halves = []
        for g in range(groups):
            slot = lax.axis_index("gy") ^ g
            position = jnp.int32(0)
            for p, j in enumerate(order):
                position = jnp.where(slot == j, p, position)
            piece = pieces_ref[position][b : b + 1]
            for h in range(per):
                q_ref[g * per + h : g * per + h + 1] = piece[:, h * DH : (h + 1) * DH]
            halves.append(piece[:, query_cols:])
        keyval = jnp.concatenate(halves, axis=1)
        new_key, new_value = keyval[:, :DH], keyval[:, DH:]
        query = q_ref[...]
        scores = lax.dot_general(
            query.astype(BF16), k_ref[b], (((1,), (1,)), ((), ())), preferred_element_type=F32
        ) * scale
        score_new = jnp.sum(query * new_key, axis=1, keepdims=True) * scale
        mask = lax.broadcasted_iota(jnp.int32, (heads, cache), 1) < lengths_ref[b]
        top = jnp.maximum(jnp.max(jnp.where(mask, scores, -1e30), axis=1, keepdims=True), score_new)
        exponent = jnp.where(mask, jnp.exp(scores - top), 0.0)
        exponent_new = jnp.exp(score_new - top)
        total = jnp.sum(exponent, axis=1, keepdims=True) + exponent_new
        weights = (exponent / total).astype(BF16)
        weights_new = (exponent_new / total).astype(BF16).astype(F32)
        contexts.append(matmul(weights, v_ref[b]) + weights_new * new_value)
    for h in range(heads):
        both = jnp.concatenate([c[h : h + 1] for c in contexts], axis=0)
        out_ref[:, h * DH : (h + 1) * DH] = both.astype(BF16)


def attention(own, arrived, k_cache, v_cache, lengths, order, after=()):
    rows, cache, _ = k_cache.shape
    return pl.pallas_call(
        functools.partial(attention_kernel, order),
        out_shape=shape((rows, HEADS * DH), BF16),
        in_specs=[SMEM, VMEM, VMEM, VMEM, VMEM] + [ANY] * len(after),
        out_specs=VMEM,
        scratch_shapes=[pltpu.VMEM((HEADS, DH), F32), pltpu.VMEM((len(order), rows, own.shape[3]), F32)],
        cost_estimate=pl.CostEstimate(
            flops=4 * rows * HEADS * cache * DH, bytes_accessed=4 * rows * cache * DH, transcendentals=0
        ),
        compiler_params=pltpu.CompilerParams(vmem_limit_bytes=6 << 20),
        name="attention",
    )(lengths, own, arrived, k_cache, v_cache, *after)


def body(stream, norm_gain, w_gate, w_up, w_query, w_keyval, k_cache, v_cache, lengths):
    size, groups = lax.axis_size("gx"), lax.axis_size("gy")
    ff = w_gate.shape[1]
    wide = w_query.shape[1] + w_keyval.shape[1]
    flat = [p for group in PORTIONS for p in group]
    tile = max(t for t in range(128, TILE + 1, 128) if ff % t == 0 and ff // t >= sum(flat))
    blocks = ff // tile
    edges = [round(blocks * sum(flat[:i]) / sum(flat)) for i in range(len(flat) + 1)]

    pieces = [[] for _ in flat]

    def swap_and_fetch(send, keep, axis, bit):
        arrived = swap(send, axis, bit)
        taken = [sum(p.shape[1] for p in held) // tile for held in pieces]
        left = [edges[i + 1] - edges[i] - taken[i] for i in range(len(flat))]
        portion = max(range(len(flat)), key=lambda i: left[i])
        count = min(AHEAD, left[portion])
        if count:
            piece = fetch(w_gate, (edges[portion] + taken[portion]) * tile, count * tile, send)
            piece, keep = lax.optimization_barrier((piece, keep))
            pieces[portion].append(piece)
        return keep, arrived

    bits = bits_of(size)
    keep, send = normalise(stream, norm_gain, size)
    for bit in bits[:-1]:
        keep, arrived = swap_and_fetch(send, keep, "gx", bit)
        send, keep = join(keep, arrived, range(1, keep.shape[0], 2))
    keep, arrived = swap_and_fetch(send, keep, "gx", bits[-1])
    (x,) = join(keep, arrived, ())
    order = [0]
    for bit in bits_of(groups)[::-1]:
        keep, arrived = swap_and_fetch(x, x, "gy", bit)
        x = jnp.concatenate([keep, arrived], axis=0)
        order = order + [j ^ bit for j in order]

    ways = [[] for _ in PORTIONS]
    group_of = [g for g, group in enumerate(PORTIONS) for _ in group]
    left = [list(bits[1:]) for _ in PORTIONS]
    hidden = [None for _ in PORTIONS]
    gather = bits_of(groups)[:0:-1]
    context = None
    arrived = []
    after = ()
    for step in ORDER:
        what, i = step[0], int(step[1:] or 0)
        if what == "K":
            first, count = edges[i], edges[i + 1] - edges[i]
            heads = () if i else (w_query, w_keyval)
            after += tuple(arrived[i - 2 : i - 1]) if i > 1 else ()
            *moved, send, keep = partials(
                x, w_gate, w_up, pieces[i], size, tile, first, count, heads, None if i else tuple(order), after
            )
            x = moved[0] if moved else x
            arrived.append(swap(send, "gx", bits[0]))
            ways[group_of[i]].append((keep, arrived[-1]))
        elif what == "S" or what == "F":
            columns = 0 if i else wide
            while left[i]:
                bit = left[i].pop(0)
                send, keep = combine(ways[i], columns, after)
                ways[i] = [(keep, swap(send, "gx", bit))]
                after = (keep,)
                if what == "S":
                    break
            if what == "F":
                earlier = hidden[:i] if i == len(PORTIONS) - 1 else []
                *parted, keep = finish(*ways[i][0], columns, groups, earlier, after)
                hidden[i] = keep
                if parted:
                    query = (parted[1], swap(parted[0], "gy", 1 << len(gather)))
        elif what == "J":
            for bit in gather:
                own, other = query
                send, keep = join(own, other, range(own.shape[0] // 2, own.shape[0]), after)
                query = (keep, swap(send, "gy", bit // 2))
                after = (keep,)
        else:
            context = attention(*query, k_cache, v_cache, lengths, tuple(order), after)
            continue
        after = (keep,)
    return hidden[-1], context


def solution(mesh):
    return jax.shard_map(
        body,
        mesh=mesh,
        in_specs=(
            P(("gx", "gy"), None),
            P(),
            P("gx", "gy"),
            P("gx", "gy"),
            P("gx", "gy"),
            P("gx", "gy"),
            P(("gx", "gy"), None, None),
            P(("gx", "gy"), None, None),
            P(("gx", "gy")),
        ),
        out_specs=(P("gx", "gy"), P(("gx", "gy"), None)),
        check_vma=False,
    )
```

```python
import functools

import jax
import jax.numpy as jnp
from jax import lax
from jax.experimental import pallas as pl
from jax.experimental.pallas import tpu as pltpu
from jax.sharding import PartitionSpec as P

HEADS = 24
DH = 256
EPS = 1e-05
PORTIONS = ((1,), (4,), (4,), (3,))
ORDER = (
    "K0", "K1", "S0", "K2", "S0", "S1", "K3", "S2", "F0", "S1", "J", "S3", "S2", "A", "S3", "F1",
    "F2", "F3",
)
TILE = 768
AHEAD = 2
SLOTS = 3
WEIGHT = 2 * 10**9

BF16 = jnp.bfloat16
F32 = jnp.float32
VMEM = pl.BlockSpec(memory_space=pltpu.VMEM)
HBM = pl.BlockSpec(memory_space=pltpu.HBM)
ANY = pl.BlockSpec(memory_space=pl.ANY)
SMEM = pl.BlockSpec(memory_space=pltpu.SMEM)


def shape(dims, dtype):
    return jax.ShapeDtypeStruct(tuple(dims), dtype)


def matmul(a, b):
    return jnp.dot(a, b, preferred_element_type=F32)


def in_hbm(x):
    return pltpu.with_memory_space_constraint(x, pltpu.HBM)


def in_vmem(x):
    return pltpu.with_memory_space_constraint(x, pltpu.VMEM)


def swap(x, axis, bit):
    size = lax.axis_size(axis)
    return lax.ppermute(x, axis, [(i, i ^ bit) for i in range(size)])


def bits_of(size):
    return [1 << t for t in range(size.bit_length() - 1)]


def norm_kernel(blocks, x_hbm, gain_hbm, keep_ref, send_ref, x_ref, gain_ref, sems):
    copies = [
        pltpu.make_async_copy(source, target, sems.at[i])
        for i, (source, target) in enumerate(((x_hbm, x_ref), (gain_hbm, gain_ref)))
    ]
    for copy in copies:
        copy.start()
    copies[0].wait()
    values = x_ref[...].astype(F32)
    width = values.shape[1]
    mean = jnp.sum(values, axis=1, keepdims=True) / width
    centred = values - mean
    variance = jnp.sum(centred * centred, axis=1, keepdims=True) / width
    root = jnp.sqrt(variance + EPS)
    part = width // blocks
    copies[1].wait()
    for k in range(blocks):
        start = pl.multiple_of((lax.axis_index("gx") ^ k) * part, 128)
        piece = x_ref[:, pl.ds(start, part)].astype(F32)
        normed = ((piece - mean) / root * gain_ref[:, pl.ds(start, part)]).astype(BF16)
        (send_ref if k % 2 else keep_ref)[k // 2, 0] = normed


def normalise(stream, norm_gain, blocks):
    rows, width = stream.shape
    out = shape((blocks // 2, 1, rows, width // blocks), BF16)
    return pl.pallas_call(
        functools.partial(norm_kernel, blocks),
        out_shape=(out, out),
        in_specs=[HBM, HBM],
        out_specs=(VMEM, VMEM),
        scratch_shapes=[
            pltpu.VMEM((rows, width), BF16),
            pltpu.VMEM((1, width), F32),
            pltpu.SemaphoreType.DMA((2,)),
        ],
        cost_estimate=pl.CostEstimate(flops=20 * 10**9, bytes_accessed=10**6, transcendentals=0),
        compiler_params=pltpu.CompilerParams(vmem_limit_bytes=2 << 20),
        name="layer_norm",
    )(in_hbm(stream), in_hbm(norm_gain.reshape(1, width)))


def join_kernel(sent, keep_ref, arrived_ref, *refs):
    slots, count = keep_ref.shape[:2]
    outs = refs[-1:] if slots == 1 else refs[-2:]
    if slots == 1:
        pieces = [ref[0, i].astype(F32) for ref in (keep_ref, arrived_ref) for i in range(count)]
        outs[0][...] = jnp.concatenate(pieces, axis=0).astype(BF16)
        return
    send_out, keep_out = outs
    places = [0, 0]
    for s in range(slots):
        way = s in sent
        out = send_out if way else keep_out
        for i in range(count):
            out[places[way], i] = keep_ref[s, i]
            out[places[way], count + i] = arrived_ref[s, i]
        places[way] += 1


def join(keep, arrived, sent, after=()):
    slots, count, rows, cols = keep.shape
    if slots == 1:
        out_shape = (shape((2 * count * rows, cols), BF16),)
    else:
        out_shape = (shape((slots // 2, 2 * count, rows, cols), BF16),) * 2
    return pl.pallas_call(
        functools.partial(join_kernel, tuple(sent)),
        out_shape=out_shape,
        in_specs=[VMEM, VMEM] + [ANY] * len(after),
        out_specs=(VMEM,) * len(out_shape),
        compiler_params=pltpu.CompilerParams(vmem_limit_bytes=2 << 20),
        cost_estimate=pl.CostEstimate(flops=WEIGHT, bytes_accessed=10**6, transcendentals=0),
        name="join_%d_%d" % (slots, cols),
    )(keep, arrived, *after)


def split(value):
    high = value.astype(BF16).astype(F32)
    return jnp.concatenate([high, value - high], axis=0).astype(BF16)


def heads_part(slots, order, x_ref, wq_ref, wkv_ref, x_out, send_ref, keep_ref):
    total = x_ref.shape[0]
    groups = len(order)
    per = total // (groups * slots)
    row = lax.broadcasted_iota(jnp.int32, (total, total), 0)
    col = lax.broadcasted_iota(jnp.int32, (total, total), 1)
    base = (row // (per * groups)) * per + row % per
    slot = (row // per) % groups
    x = x_ref[...]

    def placed(want):
        source = jnp.zeros_like(row)
        for position, j in enumerate(order):
            source = jnp.where(want == j, position * (slots * per) + base, source)
        return matmul((col == source).astype(BF16), x).astype(BF16)

    x_out[...] = placed(slot ^ lax.axis_index("gy"))
    relative = placed(slot)
    both = groups * per
    at = 0
    for w_ref in (wq_ref, wkv_ref):
        lanes = slice(at, at + w_ref.shape[1])
        part = matmul(relative, w_ref[...])
        for k in range(slots):
            mine = part[k * both : (k + 1) * both]
            if k % 2:
                send_ref[k // 2, :, lanes] = split(mine)
            else:
                keep_ref[k // 2, :, lanes] = jnp.concatenate([mine, jnp.zeros_like(mine)], axis=0)
        at += w_ref.shape[1]
    return at


def fetch_kernel(first, w_ref, after_ref, out_ref, sem):
    copy = pltpu.make_async_copy(w_ref.at[:, pl.ds(first, out_ref.shape[1])], out_ref, sem)
    copy.start()
    copy.wait()


def fetch(weights, first, cols, after):
    depth = weights.shape[0]
    return pl.pallas_call(
        functools.partial(fetch_kernel, first),
        out_shape=pltpu.VMEM((depth, cols), BF16),
        in_specs=[HBM, ANY],
        out_specs=VMEM,
        scratch_shapes=[pltpu.SemaphoreType.DMA],
        cost_estimate=pl.CostEstimate(flops=0, bytes_accessed=2 * depth * cols, transcendentals=0),
        compiler_params=pltpu.CompilerParams(vmem_limit_bytes=1 << 20),
        name="fetch_%d" % first,
    )(in_hbm(weights), after)


def partials_kernel(slots, first, count, tile, ready, order, *refs):
    x_ref, gate_ref, up_ref = refs[:3]
    resident = []
    for piece in refs[3 : 3 + ready]:
        resident += [piece.at[:, pl.ds(i * tile, tile)] for i in range(piece.shape[1] // tile)]
    held, gates, sems = refs[-3:]
    rest = refs[3 + ready : -3]
    rows = x_ref.shape[0] // slots
    room = held.shape[0]
    sources = []
    for step in range(count):
        columns = pl.ds((first + step) * tile, tile)
        if step >= len(resident):
            sources.append(gate_ref.at[:, columns])
        sources.append(up_ref.at[:, columns])
    copies = [pltpu.make_async_copy(source, held.at[i % room], sems.at[i % room]) for i, source in enumerate(sources)]
    for copy in copies[:room]:
        copy.start()
    if order is None:
        send_ref, keep_ref = rest[-2:]
        base = 0
        x = x_ref[...]
    else:
        wq_ref, wkv_ref = rest[:2]
        x_out, send_ref, keep_ref = rest[-3:]
        base = heads_part(slots, order, x_ref, wq_ref, wkv_ref, x_out, send_ref, keep_ref)
        x = x_out[...]
    at = 0

    def from_stream():
        nonlocal at
        copies[at].wait()
        out = matmul(x, held[at % room])
        if at + room < len(copies):
            copies[at + room].start()
        at += 1
        return out

    if resident:
        gates[0] = matmul(x, resident[0][...])
    for step in range(count):
        if step + 1 < len(resident):
            gates[(step + 1) % 2] = matmul(x, resident[step + 1][...])
        gate = gates[step % 2] if step < len(resident) else from_stream()
        up = from_stream()
        lanes = slice(base + step * tile, base + (step + 1) * tile)
        for k in range(slots):
            mine = slice(k * rows, (k + 1) * rows)
            both = jnp.concatenate([gate[mine], up[mine]], axis=0)
            ref = send_ref if k % 2 else keep_ref
            ref[k // 2, :, lanes] = both.astype(ref.dtype)


def partials(x, w_gate, w_up, pieces, slots, tile, first, count, heads=(), order=None, after=()):
    total, depth = x.shape
    cols = count * tile + sum(w.shape[1] for w in heads)
    out_shape = [shape(x.shape, BF16)] if heads else []
    dims = (slots // 2, 2 * total // slots, cols)
    out_shape += [shape(dims, BF16), shape(dims, F32)]
    room = max(1, min(SLOTS, 2 * count - sum(p.shape[1] for p in pieces) // tile))
    return pl.pallas_call(
        functools.partial(partials_kernel, slots, first, count, tile, len(pieces), order),
        out_shape=tuple(out_shape),
        in_specs=[VMEM, HBM, HBM] + [VMEM] * (len(pieces) + len(heads)) + [ANY] * len(after),
        out_specs=(VMEM,) * len(out_shape),
        scratch_shapes=[
            pltpu.VMEM((room, depth, tile), BF16),
            pltpu.VMEM((2, total, tile), F32),
            pltpu.SemaphoreType.DMA((room,)),
        ],
        cost_estimate=pl.CostEstimate(
            flops=4 * total * depth * cols, bytes_accessed=4 * depth * cols, transcendentals=0
        ),
        compiler_params=pltpu.CompilerParams(vmem_limit_bytes=2 * room * depth * tile + (3 << 20)),
        name="partials_%d" % first,
    )(x, in_hbm(w_gate), in_hbm(w_up), *[in_vmem(w) for w in (*pieces, *heads)], *after)


def combine_kernel(wide, count, *refs):
    send_ref, keep_ref = refs[-2:]
    at = 0
    for keep, arrived in zip(refs[: 2 * count : 2], refs[1 : 2 * count : 2]):
        for s in range(keep.shape[0]):
            both = keep[s] + arrived[s].astype(F32)
            lanes = slice(at, at + keep.shape[2])
            if s % 2 == 0:
                keep_ref[s // 2, :, lanes] = both
                continue
            send_ref[s // 2, :, lanes] = both.astype(BF16)
            if at == 0 and wide:
                rows = both.shape[0] // 2
                send_ref[s // 2, :, :wide] = split(both[:rows, :wide] + both[rows:, :wide])
        at += keep.shape[2]


def combine(parts, wide, after=()):
    slots, rows, _ = parts[0][0].shape
    cols = sum(keep.shape[2] for keep, _ in parts)
    dims = (slots // 2, rows, cols)
    return pl.pallas_call(
        functools.partial(combine_kernel, wide, len(parts)),
        out_shape=(shape(dims, BF16), shape(dims, F32)),
        in_specs=[VMEM] * (2 * len(parts)) + [ANY] * len(after),
        out_specs=(VMEM, VMEM),
        compiler_params=pltpu.CompilerParams(vmem_limit_bytes=2 << 20),
        cost_estimate=pl.CostEstimate(flops=WEIGHT, bytes_accessed=10**6, transcendentals=0),
        name="combine_%d" % cols,
    )(*[a for part in parts for a in part], *after)


def finish_kernel(wide, ready, keep_ref, arrived_ref, *refs):
    both = keep_ref[0] + arrived_ref[0].astype(F32)
    rows = both.shape[0] // 2
    if wide:
        send_ref, own_ref, hidden_ref = refs[-3:]
        middle, _, per, _ = own_ref.shape
        heads = both[:rows, :wide] + both[rows:, :wide]
        for j in range(2 * middle):
            piece = heads[j * per : (j + 1) * per].astype(BF16)
            (own_ref if j < middle else send_ref)[j % middle, 0] = piece
    else:
        hidden_ref = refs[-1]
    at = 0
    for ref in refs[:ready]:
        hidden_ref[:, at : at + ref.shape[1]] = ref[...]
        at += ref.shape[1]
    gate, up = both[:rows, wide:], both[rows:, wide:]
    hidden_ref[:, at:] = (gate * (1.0 / (1.0 + jnp.exp(-gate))) * up).astype(BF16)


def finish(keep, arrived, wide, groups, earlier, after=()):
    _, rows, cols = keep.shape
    out = [shape((rows // 2, cols - wide + sum(e.shape[1] for e in earlier)), BF16)]
    if wide:
        out = [shape((groups // 2, 1, rows // 2 // groups, wide), BF16)] * 2 + out
    return pl.pallas_call(
        functools.partial(finish_kernel, wide, len(earlier)),
        out_shape=tuple(out),
        in_specs=[VMEM] * (2 + len(earlier)) + [ANY] * len(after),
        out_specs=(VMEM,) * len(out),
        compiler_params=pltpu.CompilerParams(vmem_limit_bytes=4 << 20),
        cost_estimate=pl.CostEstimate(flops=WEIGHT, bytes_accessed=10**6, transcendentals=0),
        name="finish_%d" % cols,
    )(keep, arrived, *earlier, *after)


def attention_kernel(order, lengths_ref, own_ref, arrived_ref, k_ref, v_ref, *refs):
    out_ref, q_ref, pieces_ref = refs[-3:]
    rows, cache, _ = k_ref.shape
    groups = len(order)
    keyval_cols = 2 * DH // groups
    query_cols = own_ref.shape[3] - keyval_cols
    per = query_cols // DH
    heads = groups * per
    scale = DH ** (-0.5)
    for i in range(groups // 2):
        pieces_ref[i] = own_ref[0, i].astype(F32)
        pieces_ref[groups // 2 + i] = arrived_ref[0, i].astype(F32)
    contexts = []
    for b in range(rows):
        halves = []
        for g in range(groups):
            slot = lax.axis_index("gy") ^ g
            position = jnp.int32(0)
            for p, j in enumerate(order):
                position = jnp.where(slot == j, p, position)
            piece = pieces_ref[position][b : b + 1]
            for h in range(per):
                q_ref[g * per + h : g * per + h + 1] = piece[:, h * DH : (h + 1) * DH]
            halves.append(piece[:, query_cols:])
        keyval = jnp.concatenate(halves, axis=1)
        new_key, new_value = keyval[:, :DH], keyval[:, DH:]
        query = q_ref[...]
        scores = lax.dot_general(
            query.astype(BF16), k_ref[b], (((1,), (1,)), ((), ())), preferred_element_type=F32
        ) * scale
        score_new = jnp.sum(query * new_key, axis=1, keepdims=True) * scale
        mask = lax.broadcasted_iota(jnp.int32, (heads, cache), 1) < lengths_ref[b]
        top = jnp.maximum(jnp.max(jnp.where(mask, scores, -1e30), axis=1, keepdims=True), score_new)
        exponent = jnp.where(mask, jnp.exp(scores - top), 0.0)
        exponent_new = jnp.exp(score_new - top)
        total = jnp.sum(exponent, axis=1, keepdims=True) + exponent_new
        weights = (exponent / total).astype(BF16)
        weights_new = (exponent_new / total).astype(BF16).astype(F32)
        contexts.append(matmul(weights, v_ref[b]) + weights_new * new_value)
    for h in range(heads):
        both = jnp.concatenate([c[h : h + 1] for c in contexts], axis=0)
        out_ref[:, h * DH : (h + 1) * DH] = both.astype(BF16)


def attention(own, arrived, k_cache, v_cache, lengths, order, after=()):
    rows, cache, _ = k_cache.shape
    return pl.pallas_call(
        functools.partial(attention_kernel, order),
        out_shape=shape((rows, HEADS * DH), BF16),
        in_specs=[SMEM, VMEM, VMEM, VMEM, VMEM] + [ANY] * len(after),
        out_specs=VMEM,
        scratch_shapes=[pltpu.VMEM((HEADS, DH), F32), pltpu.VMEM((len(order), rows, own.shape[3]), F32)],
        cost_estimate=pl.CostEstimate(
            flops=4 * rows * HEADS * cache * DH, bytes_accessed=4 * rows * cache * DH, transcendentals=0
        ),
        compiler_params=pltpu.CompilerParams(vmem_limit_bytes=6 << 20),
        name="attention",
    )(lengths, own, arrived, k_cache, v_cache, *after)


def body(stream, norm_gain, w_gate, w_up, w_query, w_keyval, k_cache, v_cache, lengths):
    size, groups = lax.axis_size("gx"), lax.axis_size("gy")
    ff = w_gate.shape[1]
    wide = w_query.shape[1] + w_keyval.shape[1]
    flat = [p for group in PORTIONS for p in group]
    tile = max(t for t in range(128, TILE + 1, 128) if ff % t == 0 and ff // t >= sum(flat))
    blocks = ff // tile
    edges = [round(blocks * sum(flat[:i]) / sum(flat)) for i in range(len(flat) + 1)]

    pieces = [[] for _ in flat]

    def swap_and_fetch(send, keep, axis, bit):
        arrived = swap(send, axis, bit)
        taken = [sum(p.shape[1] for p in held) // tile for held in pieces]
        left = [edges[i + 1] - edges[i] - taken[i] for i in range(len(flat))]
        portion = max(range(len(flat)), key=lambda i: left[i])
        count = min(1 if axis == "gy" and bit == 1 else AHEAD, left[portion])
        if count:
            piece = fetch(w_gate, (edges[portion] + taken[portion]) * tile, count * tile, send)
            piece, keep = lax.optimization_barrier((piece, keep))
            pieces[portion].append(piece)
        return keep, arrived

    bits = bits_of(size)
    keep, send = normalise(stream, norm_gain, size)
    for bit in bits[:-1]:
        keep, arrived = swap_and_fetch(send, keep, "gx", bit)
        send, keep = join(keep, arrived, range(1, keep.shape[0], 2))
    keep, arrived = swap_and_fetch(send, keep, "gx", bits[-1])
    (x,) = join(keep, arrived, ())
    order = [0]
    for bit in bits_of(groups)[::-1]:
        keep, arrived = swap_and_fetch(x, x, "gy", bit)
        x = jnp.concatenate([keep, arrived], axis=0)
        order = order + [j ^ bit for j in order]

    ways = [[] for _ in PORTIONS]
    group_of = [g for g, group in enumerate(PORTIONS) for _ in group]
    left = [list(bits[1:]) for _ in PORTIONS]
    hidden = [None for _ in PORTIONS]
    gather = bits_of(groups)[:0:-1]
    context = None
    arrived = []
    after = ()
    for step in ORDER:
        what, i = step[0], int(step[1:] or 0)
        if what == "K":
            first, count = edges[i], edges[i + 1] - edges[i]
            heads = () if i else (w_query, w_keyval)
            after += tuple(arrived[i - 2 : i - 1]) if i > 1 else ()
            *moved, send, keep = partials(
                x, w_gate, w_up, pieces[i], size, tile, first, count, heads, None if i else tuple(order), after
            )
            x = moved[0] if moved else x
            arrived.append(swap(send, "gx", bits[0]))
            ways[group_of[i]].append((keep, arrived[-1]))
        elif what == "S" or what == "F":
            columns = 0 if i else wide
            while left[i]:
                bit = left[i].pop(0)
                send, keep = combine(ways[i], columns, after)
                ways[i] = [(keep, swap(send, "gx", bit))]
                after = (keep,)
                if what == "S":
                    break
            if what == "F":
                earlier = hidden[:i] if i == len(PORTIONS) - 1 else []
                *parted, keep = finish(*ways[i][0], columns, groups, earlier, after)
                hidden[i] = keep
                if parted:
                    query = (parted[1], swap(parted[0], "gy", 1 << len(gather)))
        elif what == "J":
            for bit in gather:
                own, other = query
                send, keep = join(own, other, range(own.shape[0] // 2, own.shape[0]), after)
                query = (keep, swap(send, "gy", bit // 2))
                after = (keep,)
        else:
            context = attention(*query, k_cache, v_cache, lengths, tuple(order), after)
            continue
        after = (keep,)
    return hidden[-1], context


def solution(mesh):
    return jax.shard_map(
        body,
        mesh=mesh,
        in_specs=(
            P(("gx", "gy"), None),
            P(),
            P("gx", "gy"),
            P("gx", "gy"),
            P("gx", "gy"),
            P("gx", "gy"),
            P(("gx", "gy"), None, None),
            P(("gx", "gy"), None, None),
            P(("gx", "gy")),
        ),
        out_specs=(P("gx", "gy"), P(("gx", "gy"), None)),
        check_vma=False,
    )
```
